32 devices in a mesh: row: 8 (over y, x, core), col: 4 (over z).
Axes of the slice: x: 2, y: 2, z: 4, core: 2. Of those that a mesh axis runs over, the one named last changes fastest.
Arguments:
- source: bfloat16 [16384, 64], P(('row', 'col')), may hold values from -5 to 5, as said below
- target: bfloat16 [8192, 64], P(('col', 'row')), may hold values from -2 to 2, as said below
Outputs:
- source_potential: float32 [16384], P('row')
- target_potential: float32 [8192], P('col')
The draws below stay inside these ranges and needn't reach their ends.
Inputs may be any that keep to these rules, and one draw needn't show every extreme that they name: `source`: feature values. `target`: feature values.
All inputs are finite; a program needn't handle non-finite values.
Results may differ from the reference program's by a relative error of at most 0.0003.
Values may be sent and summed in bfloat16 or wider, within the bound.
A program may use at most 64 MiB of HBM per device.

```python
import math
import jax
import jax.numpy as jnp
from jax import lax

D = 64
HALVES = 4
SOURCES = 16384
TARGETS = 8192


def shared_values(key):
    return jnp.clip(jax.random.normal(key, (TARGETS, D), jnp.float32), -4.0, 4.0)


def draw_target(key, part):
    values = 0.25 * shared_values(key)
    return values.astype(jnp.bfloat16)


def draw_source(key, part):
    key = jax.random.fold_in(key, 3)
    drawn = jnp.clip(jax.random.normal(key, (SOURCES, D), jnp.float32), -4.0, 4.0)
    positions = jnp.arange(SOURCES)
    signs = jnp.where(jax.random.uniform(jax.random.fold_in(key, 11), (SOURCES, D), jnp.float32) < 0.5, -1.0, 1.0)
    noise = jnp.clip(jax.random.normal(jax.random.fold_in(key, 13), (SOURCES, D), jnp.float32), -4.0, 4.0)
    levels = 2.5 + 0.5 * (positions // 64 % 3).astype(jnp.float32)
    planted = 4.0 * levels[:, None] * signs + 0.4 * noise
    drawn = jnp.where((positions % 64 == 17)[:, None], planted, drawn)
    return (0.25 * drawn).astype(jnp.bfloat16)


def setup_inputs(seed: int = 0) -> dict:
    splits = jax.random.split(jax.random.key(seed), 3)
    source = draw_source(jax.random.fold_in(splits[2], 71), 0)
    target = draw_target(jax.random.fold_in(splits[2], 71), 0)
    return dict(source=source, target=target)


SCALE = 0.5


def squares(features):
    wide = features.astype(jnp.float32)
    return jnp.sum(wide * wide, axis=1)


def half_update(left_feat, left_norms, right_feat, right_norms, right_pots):
    block_rows = math.gcd(left_feat.shape[0], 512)
    blocks = left_feat.shape[0] // block_rows

    def row_block(slabs):
        pieces, piece_norms = slabs
        products = jnp.dot(pieces, right_feat.T, preferred_element_type=jnp.float32)
        scores = (right_pots[None, :] - (piece_norms[:, None] + right_norms[None, :] - 2.0 * products)) / SCALE
        highest = jnp.max(scores, axis=1)
        summed = jnp.sum(jnp.exp(scores - highest[:, None]), axis=1)
        return -SCALE * (highest + jnp.log(summed)) + SCALE * jnp.log(jnp.float32(right_feat.shape[0]))

    slabs = (left_feat.reshape(blocks, block_rows, left_feat.shape[1]), left_norms.reshape(blocks, block_rows))
    return lax.map(row_block, slabs).reshape(-1)


def reference(source, target):
    source_sq = squares(source)
    target_sq = squares(target)
    source_pot = jnp.zeros((source.shape[0],), jnp.float32)
    target_pot = jnp.zeros((target.shape[0],), jnp.float32)
    for half_step in range(HALVES):
        if half_step % 2 == 0:
            source_pot = half_update(source, source_sq, target, target_sq, target_pot)
        else:
            target_pot = half_update(target, target_sq, source, source_sq, source_pot)
    return source_pot, target_pot
```

```python
import functools
import math

import jax
import jax.numpy as jnp
from jax import lax
from jax.experimental import pallas as pl
from jax.experimental.pallas import tpu as pltpu
from jax.sharding import PartitionSpec as P

MESH = pl.DeviceIdType.MESH
CHUNK = 128
LANES = 128
NT_DIMS = (((1,), (1,)), ((), ()))


def spread(row):
    return jnp.broadcast_to(row, (CHUNK, LANES)).T


def exact_pieces(squared):
    high = squared.astype(jnp.bfloat16)
    low = (squared - high.astype(jnp.float32)).astype(jnp.bfloat16)
    return high, low


def kernel(
    row_n, col_n, src_ref, tgt_ref, spot_ref, tpot_ref,
    src_all, tgt_all, left, right, squares, block, peaks, sums, scales, column_acc, lse, source_norm, tpot_one,
    first_out, first_in, second_out, second_in, third_out, third_in, fourth_out, fourth_in,
    src_send, src_recv, tgt_send, tgt_recv, x1_send, x1_recv, x2_send, x2_recv, x3_send, x3_recv, x4_send, x4_recv,
):
    my_row, my_col = lax.axis_index("row"), lax.axis_index("col")
    src_piece, depth = src_ref.shape
    tgt_piece = tgt_ref.shape[0]
    rows, cols = src_piece * col_n, tgt_piece * row_n
    chunks, tiles = rows // CHUNK, cols // LANES
    sources_all, targets_all = rows * row_n, cols * col_n
    log_sources, log_targets = math.log(sources_all), math.log(targets_all)

    def col_peer(step):
        return (my_row, lax.rem(my_col + step, col_n))

    def row_peer(step):
        return (lax.rem(my_row + step, row_n), my_col)

    barrier = pltpu.get_barrier_semaphore()
    for step in range(1, row_n):
        pl.semaphore_signal(barrier, inc=1, device_id=row_peer(step), device_id_type=MESH)
    for step in range(1, col_n):
        pl.semaphore_signal(barrier, inc=1, device_id=col_peer(step), device_id_type=MESH)
    pl.semaphore_wait(barrier, row_n + col_n - 2)

    def broadcast(source, landing, slot, send, recv, count, peer):
        copies = []
        for step in range(1, count):
            copy = pltpu.make_async_remote_copy(
                src_ref=source,
                dst_ref=landing.at[slot],
                send_sem=send.at[step - 1],
                recv_sem=recv.at[step - 1],
                device_id=peer(step),
                device_id_type=MESH,
            )
            copy.start()
            copies.append(copy)
        return copies

    src_copies = broadcast(src_ref, src_all, my_col, src_send, src_recv, col_n, col_peer)
    tgt_copies = broadcast(tgt_ref, tgt_all, my_row, tgt_send, tgt_recv, row_n, row_peer)
    src_all[my_col] = src_ref[...]
    tgt_all[my_row] = tgt_ref[...]
    for copy in src_copies + tgt_copies:
        copy.wait()

    def build_left(piece, unused):
        wide = src_all[piece].astype(jnp.float32)
        at = pl.ds(pl.multiple_of(piece * src_piece, src_piece), src_piece)
        left[at, 0:LANES] = jnp.concatenate([4.0 * wide, jnp.full_like(wide, -2.0)], axis=1).astype(jnp.bfloat16)
        left[at, LANES : 2 * LANES] = jnp.concatenate(
            [jnp.full_like(wide, -2.0), jnp.zeros_like(wide)], axis=1
        ).astype(jnp.bfloat16)
        high, low = exact_pieces(wide * wide)
        squares[at, :] = jnp.concatenate([high.astype(jnp.float32), low.astype(jnp.float32)], axis=1).astype(
            jnp.bfloat16
        )
        return unused

    lax.fori_loop(0, col_n, build_left, 0)

    def build_right(piece, unused):
        wide = tgt_all[piece].astype(jnp.float32)
        at = pl.ds(pl.multiple_of(piece * tgt_piece, tgt_piece), tgt_piece)
        high, low = exact_pieces(wide * wide)
        right[at, 0:LANES] = jnp.concatenate([wide, high.astype(jnp.float32)], axis=1).astype(jnp.bfloat16)
        right[at, LANES : 2 * LANES] = jnp.concatenate(
            [low.astype(jnp.float32), jnp.zeros_like(wide)], axis=1
        ).astype(jnp.bfloat16)
        return unused

    lax.fori_loop(0, row_n, build_right, 0)

    def chunk_rows(chunk):
        return pl.ds(pl.multiple_of(chunk * CHUNK, CHUNK), CHUNK)

    def lanes(tile):
        return slice(tile * LANES, (tile + 1) * LANES)

    def half_zero(chunk, unused):
        at = chunk_rows(chunk)
        norm = lax.dot_general(
            jnp.ones((8, 2 * depth), jnp.bfloat16), squares[at, :], NT_DIMS, preferred_element_type=jnp.float32
        )
        source_norm[pl.ds(chunk, 1), :] = norm[0:1, :]
        block[at, :] = lax.dot_general(left[at, :], right[...], NT_DIMS, preferred_element_type=jnp.float32)
        top = block[at, lanes(0)]
        for tile in range(1, tiles):
            top = jnp.maximum(top, block[at, lanes(tile)])
        highest = jnp.max(top, axis=1, keepdims=True)
        total = jnp.exp(block[at, lanes(0)] - highest)
        for tile in range(1, tiles):
            total = total + jnp.exp(block[at, lanes(tile)] - highest)
        first_out[0, pl.ds(chunk, 1), :] = jnp.max(top.T, axis=0, keepdims=True)
        first_out[1, pl.ds(chunk, 1), :] = jnp.sum(total.T, axis=0, keepdims=True)
        return unused

    lax.fori_loop(0, chunks, half_zero, 0)
    copies = broadcast(first_out, first_in, my_col, x1_send, x1_recv, col_n, col_peer)
    first_in[my_col] = first_out[...]
    for copy in copies:
        copy.wait()
    overall = first_in[0, 0]
    for other in range(1, col_n):
        overall = jnp.maximum(overall, first_in[other, 0])
    summed = jnp.zeros_like(overall)
    for other in range(col_n):
        summed = summed + first_in[other, 1] * jnp.exp(first_in[other, 0] - overall)
    lse[...] = overall + jnp.log(summed)

    def half_one(chunk, unused):
        at = chunk_rows(chunk)
        shift = spread(lse[pl.ds(chunk, 1), :])
        for tile in range(tiles):
            shifted = block[at, lanes(tile)] - shift
            highest = jnp.max(shifted, axis=0, keepdims=True)
            value = jnp.exp(shifted - highest)
            block[at, lanes(tile)] = value
            peaks[chunk, tile : tile + 1, :] = highest
            sums[chunk, tile : tile + 1, :] = jnp.sum(value, axis=0, keepdims=True)
        return unused

    lax.fori_loop(0, chunks, half_one, 0)
    overall = peaks[0]
    for chunk in range(1, chunks):
        overall = jnp.maximum(overall, peaks[chunk])
    summed = jnp.zeros_like(overall)
    for chunk in range(chunks):
        summed = summed + sums[chunk] * jnp.exp(peaks[chunk] - overall)
    second_out[0] = overall
    second_out[1] = summed
    copies = broadcast(second_out, second_in, my_row, x2_send, x2_recv, row_n, row_peer)
    second_in[my_row] = second_out[...]
    for copy in copies:
        copy.wait()
    overall = second_in[0, 0]
    for other in range(1, row_n):
        overall = jnp.maximum(overall, second_in[other, 0])
    summed = jnp.zeros_like(overall)
    for other in range(row_n):
        summed = summed + second_in[other, 1] * jnp.exp(second_in[other, 0] - overall)
    tpot_one[...] = 0.5 * (log_sources - log_targets) - 0.5 * (overall + jnp.log(summed))
    inverse = float(sources_all) / summed
    for chunk in range(chunks):
        scales[chunk] = jnp.exp(peaks[chunk] - overall) * inverse

    def half_two(chunk, unused):
        at = chunk_rows(chunk)
        total = block[at, lanes(0)] * scales[chunk, 0:1, :]
        for tile in range(1, tiles):
            total = total + block[at, lanes(tile)] * scales[chunk, tile : tile + 1, :]
        third_out[pl.ds(chunk, 1), :] = jnp.sum(total.T, axis=0, keepdims=True)
        return unused

    lax.fori_loop(0, chunks, half_two, 0)
    copies = broadcast(third_out, third_in, my_col, x3_send, x3_recv, col_n, col_peer)
    third_in[my_col] = third_out[...]
    for copy in copies:
        copy.wait()
    summed = third_in[0]
    for other in range(1, col_n):
        summed = summed + third_in[other]
    spot_ref[...] = source_norm[...] + log_targets - 0.5 * (lse[...] + jnp.log(summed))
    lse[...] = float(targets_all) / summed

    column_acc[...] = jnp.zeros_like(column_acc)

    def half_three(chunk, unused):
        at = chunk_rows(chunk)
        weight = spread(lse[pl.ds(chunk, 1), :])
        for tile in range(tiles):
            weighted = (block[at, lanes(tile)] * weight).reshape(CHUNK // 8, 8, LANES)
            column_acc[tile] += jnp.sum(weighted, axis=0) * scales[chunk, tile : tile + 1, :]
        return unused

    lax.fori_loop(0, chunks, half_three, 0)
    fourth_out[...] = jnp.sum(column_acc[...], axis=1)
    copies = broadcast(fourth_out, fourth_in, my_row, x4_send, x4_recv, row_n, row_peer)
    fourth_in[my_row] = fourth_out[...]
    for copy in copies:
        copy.wait()
    summed = fourth_in[0]
    for other in range(1, row_n):
        summed = summed + fourth_in[other]
    tpot_ref[...] = tpot_one[...] + 0.5 * log_sources - 0.5 * jnp.log(summed)


def local(source, target):
    row_n, col_n = lax.axis_size("row"), lax.axis_size("col")
    src_piece, depth = source.shape
    tgt_piece = target.shape[0]
    rows, cols = src_piece * col_n, tgt_piece * row_n
    chunks, tiles = rows // CHUNK, cols // LANES
    f32, bf16 = jnp.float32, jnp.bfloat16
    vmem = pl.BlockSpec(memory_space=pltpu.VMEM)
    row_sems, col_sems = pltpu.SemaphoreType.DMA((row_n - 1,)), pltpu.SemaphoreType.DMA((col_n - 1,))
    spot, tpot = pl.pallas_call(
        functools.partial(kernel, row_n, col_n),
        out_shape=(
            jax.ShapeDtypeStruct((chunks, LANES), f32),
            jax.ShapeDtypeStruct((tiles, LANES), f32),
        ),
        in_specs=[vmem, vmem],
        out_specs=(vmem, vmem),
        scratch_shapes=[
            pltpu.VMEM((col_n, src_piece, depth), bf16),
            pltpu.VMEM((row_n, tgt_piece, depth), bf16),
            pltpu.VMEM((rows, 2 * LANES), bf16),
            pltpu.VMEM((cols, 2 * LANES), bf16),
            pltpu.VMEM((rows, 2 * depth), bf16),
            pltpu.VMEM((rows, cols), f32),
            pltpu.VMEM((chunks, tiles, LANES), f32),
            pltpu.VMEM((chunks, tiles, LANES), f32),
            pltpu.VMEM((chunks, tiles, LANES), f32),
            pltpu.VMEM((tiles, 8, LANES), f32),
            pltpu.VMEM((chunks, LANES), f32),
            pltpu.VMEM((chunks, LANES), f32),
            pltpu.VMEM((tiles, LANES), f32),
            pltpu.VMEM((2, chunks, LANES), f32),
            pltpu.VMEM((col_n, 2, chunks, LANES), f32),
            pltpu.VMEM((2, tiles, LANES), f32),
            pltpu.VMEM((row_n, 2, tiles, LANES), f32),
            pltpu.VMEM((chunks, LANES), f32),
            pltpu.VMEM((col_n, chunks, LANES), f32),
            pltpu.VMEM((tiles, LANES), f32),
            pltpu.VMEM((row_n, tiles, LANES), f32),
            col_sems, col_sems, row_sems, row_sems,
            col_sems, col_sems, row_sems, row_sems,
            col_sems, col_sems, row_sems, row_sems,
        ],
        compiler_params=pltpu.CompilerParams(
            collective_id=0, has_side_effects=True, vmem_limit_bytes=48 * 1024 * 1024
        ),
    )(source, target)
    return spot.reshape(-1), tpot.reshape(-1)


def solution(mesh):
    placed = (P(("row", "col"), None), P(("col", "row"), None))
    return jax.shard_map(
        local, mesh=mesh, in_specs=placed, out_specs=(P("row"), P("col")), check_vma=False
    )
```

```python
import functools
import math

import jax
import jax.numpy as jnp
from jax import lax
from jax.experimental import pallas as pl
from jax.experimental.pallas import tpu as pltpu
from jax.sharding import PartitionSpec as P

MESH = pl.DeviceIdType.MESH
CHUNK = 128
LANES = 128
NN_DIMS = (((1,), (0,)), ((), ()))


def spread(row):
    return jnp.broadcast_to(row, (CHUNK, LANES)).T


def exact_pieces(squared):
    high = squared.astype(jnp.bfloat16)
    low = (squared - high.astype(jnp.float32)).astype(jnp.bfloat16)
    return high, low


def kernel(
    row_n, col_n, src_ref, tgt_ref, spot_ref, tpot_ref,
    src_all, tgt_all, left, right, tops, block, peaks, sums, scales, column_acc, lse, source_norm, tpot_one,
    first_out, first_in, second_out, second_in, third_out, third_in, fourth_out, fourth_in,
    src_send, src_recv, tgt_send, tgt_recv, x1_send, x1_recv, x2_send, x2_recv, x3_send, x3_recv, x4_send, x4_recv,
):
    my_row, my_col = lax.axis_index("row"), lax.axis_index("col")
    depth, src_piece = src_ref.shape
    tgt_piece = tgt_ref.shape[1]
    rows, cols = src_piece * col_n, tgt_piece * row_n
    chunks, tiles = rows // CHUNK, cols // LANES
    sources_all, targets_all = rows * row_n, cols * col_n
    log_sources, log_targets = math.log(sources_all), math.log(targets_all)

    def col_peer(step):
        return (my_row, lax.rem(my_col + step, col_n))

    def row_peer(step):
        return (lax.rem(my_row + step, row_n), my_col)

    barrier = pltpu.get_barrier_semaphore()
    for step in range(1, row_n):
        pl.semaphore_signal(barrier, inc=1, device_id=row_peer(step), device_id_type=MESH)
    for step in range(1, col_n):
        pl.semaphore_signal(barrier, inc=1, device_id=col_peer(step), device_id_type=MESH)
    pl.semaphore_wait(barrier, row_n + col_n - 2)

    def broadcast(source, landing, slot, send, recv, count, peer):
        copies = []
        for step in range(1, count):
            copy = pltpu.make_async_remote_copy(
                src_ref=source,
                dst_ref=landing.at[slot],
                send_sem=send.at[step - 1],
                recv_sem=recv.at[step - 1],
                device_id=peer(step),
                device_id_type=MESH,
            )
            copy.start()
            copies.append(copy)
        return copies

    def send_all(source, target, send, recv, count, peer):
        copies = []
        for step in range(1, count):
            copy = pltpu.make_async_remote_copy(
                src_ref=source,
                dst_ref=target,
                send_sem=send(step - 1),
                recv_sem=recv,
                device_id=peer(step),
                device_id_type=MESH,
            )
            copy.start()
            copies.append(copy)
        return copies

    tgt_copies = broadcast(tgt_ref, tgt_all, my_row, tgt_send, tgt_recv, row_n, row_peer)
    src_copies = send_all(
        src_ref, src_all.at[my_col], lambda k: src_send.at[k], src_recv.at[my_col], col_n, col_peer
    )
    src_all[my_col] = src_ref[...]
    tgt_all[my_row] = tgt_ref[...]
    left[:, depth : 3 * depth] = jnp.full((rows, 2 * depth), -2.0, jnp.bfloat16)
    for copy in tgt_copies:
        copy.wait()

    for piece in range(row_n):
        wide = tgt_all[piece].astype(jnp.float32)
        high, low = exact_pieces(wide * wide)
        at = slice(piece * tgt_piece, (piece + 1) * tgt_piece)
        right[0:depth, at] = tgt_all[piece]
        right[depth : 2 * depth, at] = high
        right[2 * depth : 3 * depth, at] = low

    def chunk_rows(chunk):
        return pl.ds(pl.multiple_of(chunk * CHUNK, CHUNK), CHUNK)

    def lanes(tile):
        return slice(tile * LANES, (tile + 1) * LANES)

    piece_chunks = src_piece // CHUNK
    width = math.gcd(cols, 512)

    def half_zero(piece):
        wide = src_all[piece].astype(jnp.float32)
        at = pl.ds(pl.multiple_of(piece * src_piece, src_piece), src_piece)
        left[at, 0:depth] = (4.0 * wide).T.astype(jnp.bfloat16)
        norm = jnp.sum(wide * wide, axis=0, keepdims=True)
        for part in range(piece_chunks):
            source_norm[pl.ds(piece * piece_chunks + part, 1), :] = norm[:, lanes(part)]
        top = None
        for group in range(cols // width):
            at_cols = slice(group * width, (group + 1) * width)
            score = lax.dot_general(
                left[at, :], right[:, at_cols], NN_DIMS, preferred_element_type=jnp.float32
            )
            block[at, at_cols] = score
            for tile in range(width // LANES):
                part = score[:, lanes(tile)]
                top = part if top is None else jnp.maximum(top, part)
        tops[...] = top

        def exponentials(part, unused):
            at = chunk_rows(piece * piece_chunks + part)
            top = tops[chunk_rows(part), :]
            highest = jnp.max(top, axis=1, keepdims=True)
            total = jnp.exp(block[at, lanes(0)] - highest)
            for tile in range(1, tiles):
                total = total + jnp.exp(block[at, lanes(tile)] - highest)
            first_out[piece, 0, pl.ds(part, 1), :] = jnp.max(top.T, axis=0, keepdims=True)
            first_out[piece, 1, pl.ds(part, 1), :] = jnp.sum(total.T, axis=0, keepdims=True)
            return unused

        lax.fori_loop(0, piece_chunks, exponentials, 0)
        send_all(
            first_out.at[piece], first_in.at[my_col, piece],
            lambda k: x1_send.at[k, piece], x1_recv.at[my_col, piece], col_n, col_peer,
        )
        first_in[my_col, piece] = first_out[piece]

    half_zero(my_col)

    def other_piece(step, unused):
        piece = step + lax.div(step - my_col + col_n, col_n)
        pltpu.make_async_remote_copy(
            src_ref=src_ref,
            dst_ref=src_all.at[piece],
            send_sem=src_send.at[0],
            recv_sem=src_recv.at[piece],
            device_id=col_peer(1),
            device_id_type=MESH,
        ).wait_recv()
        half_zero(piece)
        return unused

    lax.fori_loop(0, col_n - 1, other_piece, 0)
    for copy in src_copies:
        copy.wait_send()

    def first_copy(step, sender, piece):
        return pltpu.make_async_remote_copy(
            src_ref=first_out.at[piece],
            dst_ref=first_in.at[sender, piece],
            send_sem=x1_send.at[step - 1, piece],
            recv_sem=x1_recv.at[sender, piece],
            device_id=col_peer(step),
            device_id_type=MESH,
        )

    def finish_rows(piece, unused):
        for step in range(1, col_n):
            first_copy(step, lax.rem(my_col + step, col_n), piece).wait()
        overall = first_in[0, piece, 0]
        for other in range(1, col_n):
            overall = jnp.maximum(overall, first_in[other, piece, 0])
        summed = jnp.zeros_like(overall)
        for other in range(col_n):
            summed = summed + first_in[other, piece, 1] * jnp.exp(first_in[other, piece, 0] - overall)
        total = overall + jnp.log(summed)
        for part in range(piece_chunks):
            lse[pl.ds(piece * piece_chunks + part, 1), :] = total[part : part + 1, :]
        lax.fori_loop(piece * piece_chunks, (piece + 1) * piece_chunks, half_one, 0)
        return unused

    def half_one(chunk, unused):
        at = chunk_rows(chunk)
        shift = spread(lse[pl.ds(chunk, 1), :])
        for tile in range(tiles):
            shifted = block[at, lanes(tile)] - shift
            highest = jnp.max(shifted, axis=0, keepdims=True)
            value = jnp.exp(shifted - highest)
            block[at, lanes(tile)] = value
            peaks[chunk, tile : tile + 1, :] = highest
            sums[chunk, tile : tile + 1, :] = jnp.sum(value, axis=0, keepdims=True)
        return unused

    lax.fori_loop(0, col_n, finish_rows, 0)
    overall = peaks[0]
    for chunk in range(1, chunks):
        overall = jnp.maximum(overall, peaks[chunk])
    summed = jnp.zeros_like(overall)
    for chunk in range(chunks):
        summed = summed + sums[chunk] * jnp.exp(peaks[chunk] - overall)
    second_out[0] = overall
    second_out[1] = summed
    copies = broadcast(second_out, second_in, my_row, x2_send, x2_recv, row_n, row_peer)
    second_in[my_row] = second_out[...]
    for copy in copies:
        copy.wait()
    overall = second_in[0, 0]
    for other in range(1, row_n):
        overall = jnp.maximum(overall, second_in[other, 0])
    summed = jnp.zeros_like(overall)
    for other in range(row_n):
        summed = summed + second_in[other, 1] * jnp.exp(second_in[other, 0] - overall)
    tpot_one[...] = 0.5 * (log_sources - log_targets) - 0.5 * (overall + jnp.log(summed))
    inverse = float(sources_all) / summed
    for chunk in range(chunks):
        scales[chunk] = jnp.exp(peaks[chunk] - overall) * inverse

    def half_two(chunk, unused):
        at = chunk_rows(chunk)
        total = block[at, lanes(0)] * scales[chunk, 0:1, :]
        for tile in range(1, tiles):
            total = total + block[at, lanes(tile)] * scales[chunk, tile : tile + 1, :]
        third_out[pl.ds(chunk, 1), :] = jnp.sum(total.T, axis=0, keepdims=True)
        return unused

    lax.fori_loop(0, chunks, half_two, 0)
    copies = broadcast(third_out, third_in, my_col, x3_send, x3_recv, col_n, col_peer)
    third_in[my_col] = third_out[...]
    for copy in copies:
        copy.wait()
    summed = third_in[0]
    for other in range(1, col_n):
        summed = summed + third_in[other]
    spot_ref[...] = source_norm[...] + log_targets - 0.5 * (lse[...] + jnp.log(summed))
    lse[...] = float(targets_all) / summed

    column_acc[...] = jnp.zeros_like(column_acc)

    def half_three(chunk, unused):
        at = chunk_rows(chunk)
        weight = spread(lse[pl.ds(chunk, 1), :])
        for tile in range(tiles):
            weighted = (block[at, lanes(tile)] * weight).reshape(CHUNK // 8, 8, LANES)
            column_acc[tile] += jnp.sum(weighted, axis=0) * scales[chunk, tile : tile + 1, :]
        return unused

    lax.fori_loop(0, chunks, half_three, 0)
    fourth_out[...] = jnp.sum(column_acc[...], axis=1)
    copies = broadcast(fourth_out, fourth_in, my_row, x4_send, x4_recv, row_n, row_peer)
    fourth_in[my_row] = fourth_out[...]
    for copy in copies:
        copy.wait()
    summed = fourth_in[0]
    for other in range(1, row_n):
        summed = summed + fourth_in[other]
    tpot_ref[...] = tpot_one[...] + 0.5 * log_sources - 0.5 * jnp.log(summed)


def local(source, target):
    row_n, col_n = lax.axis_size("row"), lax.axis_size("col")
    src_piece, depth = source.shape
    tgt_piece = target.shape[0]
    rows, cols = src_piece * col_n, tgt_piece * row_n
    chunks, tiles = rows // CHUNK, cols // LANES
    f32, bf16 = jnp.float32, jnp.bfloat16
    vmem = pl.BlockSpec(memory_space=pltpu.VMEM)
    row_sems, col_sems = pltpu.SemaphoreType.DMA((row_n - 1,)), pltpu.SemaphoreType.DMA((col_n - 1,))
    spot, tpot = pl.pallas_call(
        functools.partial(kernel, row_n, col_n),
        out_shape=(
            jax.ShapeDtypeStruct((chunks, LANES), f32),
            jax.ShapeDtypeStruct((tiles, LANES), f32),
        ),
        in_specs=[vmem, vmem],
        out_specs=(vmem, vmem),
        scratch_shapes=[
            pltpu.VMEM((col_n, depth, src_piece), bf16),
            pltpu.VMEM((row_n, depth, tgt_piece), bf16),
            pltpu.VMEM((rows, 3 * depth), bf16),
            pltpu.VMEM((3 * depth, cols), bf16),
            pltpu.VMEM((src_piece, LANES), f32),
            pltpu.VMEM((rows, cols), f32),
            pltpu.VMEM((chunks, tiles, LANES), f32),
            pltpu.VMEM((chunks, tiles, LANES), f32),
            pltpu.VMEM((chunks, tiles, LANES), f32),
            pltpu.VMEM((tiles, 8, LANES), f32),
            pltpu.VMEM((chunks, LANES), f32),
            pltpu.VMEM((chunks, LANES), f32),
            pltpu.VMEM((tiles, LANES), f32),
            pltpu.VMEM((col_n, 2, src_piece // CHUNK, LANES), f32),
            pltpu.VMEM((col_n, col_n, 2, src_piece // CHUNK, LANES), f32),
            pltpu.VMEM((2, tiles, LANES), f32),
            pltpu.VMEM((row_n, 2, tiles, LANES), f32),
            pltpu.VMEM((chunks, LANES), f32),
            pltpu.VMEM((col_n, chunks, LANES), f32),
            pltpu.VMEM((tiles, LANES), f32),
            pltpu.VMEM((row_n, tiles, LANES), f32),
            col_sems, pltpu.SemaphoreType.DMA((col_n,)), row_sems, row_sems,
            pltpu.SemaphoreType.DMA((col_n - 1, col_n)), pltpu.SemaphoreType.DMA((col_n, col_n)), row_sems, row_sems,
            col_sems, col_sems, row_sems, row_sems,
        ],
        compiler_params=pltpu.CompilerParams(
            collective_id=0, has_side_effects=True, vmem_limit_bytes=48 * 1024 * 1024
        ),
    )(source.T, target.T)
    return spot.reshape(-1), tpot.reshape(-1)


def solution(mesh):
    placed = (P(("row", "col"), None), P(("col", "row"), None))
    return jax.shard_map(
        local, mesh=mesh, in_specs=placed, out_specs=(P("row"), P("col")), check_vma=False
    )
```

```python
import functools
import math

import jax
import jax.numpy as jnp
from jax import lax
from jax.experimental import pallas as pl
from jax.experimental.pallas import tpu as pltpu
from jax.sharding import PartitionSpec as P

MESH = pl.DeviceIdType.MESH
CHUNK = 128
LANES = 128
NN_DIMS = (((1,), (0,)), ((), ()))


def spread(row):
    return jnp.broadcast_to(row, (CHUNK, LANES)).T


def exact_pieces(squared):
    high = squared.astype(jnp.bfloat16)
    low = (squared - high.astype(jnp.float32)).astype(jnp.bfloat16)
    return high, low


def kernel(
    row_n, col_n, src_ref, tgt_ref, spot_ref, tpot_ref,
    src_all, tgt_all, left, right, tops, block, peaks, sums, scales, column_acc, lse, source_norm, tpot_one,
    first_out, first_in, second_out, second_in, third_out, third_in, fourth_out, fourth_in,
    src_send, src_recv, tgt_send, tgt_recv, x1_send, x1_recv, x2_send, x2_recv, x3_send, x3_recv, x4_send, x4_recv,
):
    my_row, my_col = lax.axis_index("row"), lax.axis_index("col")
    depth, src_piece = src_ref.shape
    tgt_piece = tgt_ref.shape[1]
    rows, cols = src_piece * col_n, tgt_piece * row_n
    chunks, tiles = rows // CHUNK, cols // LANES
    sources_all, targets_all = rows * row_n, cols * col_n
    log_sources, log_targets = math.log(sources_all), math.log(targets_all)

    def col_peer(step):
        return (my_row, lax.rem(my_col + step, col_n))

    def nearest(step):
        below, above = my_col, col_n - 1 - my_col
        low_side = lax.div(above - below + col_n, col_n)
        reach = low_side * below + (1 - low_side) * above
        both = lax.div(2 * reach - step + col_n, col_n)
        around = (step + 1) // 2 * (2 * (step % 2) - 1)
        return my_col + both * around + (1 - both) * (step - reach) * (2 * low_side - 1)

    def near_peer(step):
        return (my_row, nearest(step))

    def row_peer(step):
        return (lax.rem(my_row + step, row_n), my_col)

    barrier = pltpu.get_barrier_semaphore()
    for step in range(1, row_n):
        pl.semaphore_signal(barrier, inc=1, device_id=row_peer(step), device_id_type=MESH)
    for step in range(1, col_n):
        pl.semaphore_signal(barrier, inc=1, device_id=col_peer(step), device_id_type=MESH)
    src_all[my_col] = src_ref[...]
    tgt_all[my_row] = tgt_ref[...]
    left[:, depth : 3 * depth] = jnp.full((rows, 2 * depth), -2.0, jnp.bfloat16)
    pl.semaphore_wait(barrier, row_n + col_n - 2)

    def broadcast(source, landing, slot, send, recv, count, peer):
        copies = []
        for step in range(1, count):
            copy = pltpu.make_async_remote_copy(
                src_ref=source,
                dst_ref=landing.at[slot],
                send_sem=send.at[step - 1],
                recv_sem=recv.at[step - 1],
                device_id=peer(step),
                device_id_type=MESH,
            )
            copy.start()
            copies.append(copy)
        return copies

    def send_all(source, target, send, recv, count, peer):
        copies = []
        for step in range(1, count):
            copy = pltpu.make_async_remote_copy(
                src_ref=source,
                dst_ref=target,
                send_sem=send(step - 1),
                recv_sem=recv,
                device_id=peer(step),
                device_id_type=MESH,
            )
            copy.start()
            copies.append(copy)
        return copies

    src_copies = send_all(
        src_ref, src_all.at[my_col], lambda k: src_send.at[k], src_recv.at[my_col], col_n, near_peer
    )
    tgt_copies = broadcast(tgt_ref, tgt_all, my_row, tgt_send, tgt_recv, row_n, row_peer)
    for copy in tgt_copies:
        copy.wait()

    for piece in range(row_n):
        wide = tgt_all[piece].astype(jnp.float32)
        high, low = exact_pieces(wide * wide)
        at = slice(piece * tgt_piece, (piece + 1) * tgt_piece)
        right[0:depth, at] = tgt_all[piece]
        right[depth : 2 * depth, at] = high
        right[2 * depth : 3 * depth, at] = low

    def chunk_rows(chunk):
        return pl.ds(pl.multiple_of(chunk * CHUNK, CHUNK), CHUNK)

    def lanes(tile):
        return slice(tile * LANES, (tile + 1) * LANES)

    piece_chunks = src_piece // CHUNK
    width = math.gcd(cols, 512)

    def half_zero(piece):
        wide = src_all[piece].astype(jnp.float32)
        at = pl.ds(pl.multiple_of(piece * src_piece, src_piece), src_piece)
        left[at, 0:depth] = (4.0 * wide).T.astype(jnp.bfloat16)
        norm = jnp.sum(wide * wide, axis=0, keepdims=True)
        for part in range(piece_chunks):
            source_norm[pl.ds(piece * piece_chunks + part, 1), :] = norm[:, lanes(part)]
        top = None
        for group in range(cols // width):
            at_cols = slice(group * width, (group + 1) * width)
            score = lax.dot_general(
                left[at, :], right[:, at_cols], NN_DIMS, preferred_element_type=jnp.float32
            )
            block[at, at_cols] = score
            for tile in range(width // LANES):
                part = score[:, lanes(tile)]
                top = part if top is None else jnp.maximum(top, part)
        tops[...] = top

        def exponentials(part, unused):
            at = chunk_rows(piece * piece_chunks + part)
            top = tops[chunk_rows(part), :]
            highest = jnp.max(top, axis=1, keepdims=True)
            total = jnp.exp(block[at, lanes(0)] - highest)
            for tile in range(1, tiles):
                total = total + jnp.exp(block[at, lanes(tile)] - highest)
            first_out[piece, pl.ds(part, 1), :] = jnp.max(top.T, axis=0, keepdims=True) + jnp.log(
                jnp.sum(total.T, axis=0, keepdims=True)
            )
            return unused

        lax.fori_loop(0, piece_chunks, exponentials, 0)
        send_all(
            first_out.at[piece], first_in.at[my_col, piece],
            lambda k: x1_send.at[k, piece], x1_recv.at[my_col, piece], col_n, col_peer,
        )
        first_in[my_col, piece] = first_out[piece]

    half_zero(my_col)

    def other_piece(step, unused):
        piece = nearest(step)
        pltpu.make_async_remote_copy(
            src_ref=src_ref,
            dst_ref=src_all.at[piece],
            send_sem=src_send.at[0],
            recv_sem=src_recv.at[piece],
            device_id=col_peer(1),
            device_id_type=MESH,
        ).wait_recv()
        half_zero(piece)
        return unused

    lax.fori_loop(1, col_n, other_piece, 0)
    for copy in src_copies:
        copy.wait_send()

    def first_copy(step, sender, piece):
        return pltpu.make_async_remote_copy(
            src_ref=first_out.at[piece],
            dst_ref=first_in.at[sender, piece],
            send_sem=x1_send.at[step - 1, piece],
            recv_sem=x1_recv.at[sender, piece],
            device_id=col_peer(step),
            device_id_type=MESH,
        )

    def finish_rows(place, unused):
        piece = (col_n - 1) // 2 + (place + 1) // 2 * (2 * (place % 2) - 1)
        for step in range(1, col_n):
            first_copy(step, lax.rem(my_col + step, col_n), piece).wait()
        overall = first_in[0, piece]
        for other in range(1, col_n):
            overall = jnp.maximum(overall, first_in[other, piece])
        summed = jnp.zeros_like(overall)
        for other in range(col_n):
            summed = summed + jnp.exp(first_in[other, piece] - overall)
        total = overall + jnp.log(summed)
        for part in range(piece_chunks):
            lse[pl.ds(piece * piece_chunks + part, 1), :] = total[part : part + 1, :]
        lax.fori_loop(piece * piece_chunks, (piece + 1) * piece_chunks, half_one, 0)
        return unused

    def half_one(chunk, unused):
        at = chunk_rows(chunk)
        shift = spread(lse[pl.ds(chunk, 1), :])
        for tile in range(tiles):
            shifted = block[at, lanes(tile)] - shift
            highest = jnp.max(shifted, axis=0, keepdims=True)
            value = jnp.exp(shifted - highest)
            block[at, lanes(tile)] = value
            peaks[chunk, tile : tile + 1, :] = highest
            sums[chunk, tile : tile + 1, :] = jnp.sum(value, axis=0, keepdims=True)
        return unused

    lax.fori_loop(0, col_n, finish_rows, 0)
    overall = peaks[0]
    for chunk in range(1, chunks):
        overall = jnp.maximum(overall, peaks[chunk])
    summed = jnp.zeros_like(overall)
    for chunk in range(chunks):
        summed = summed + sums[chunk] * jnp.exp(peaks[chunk] - overall)
    second_out[...] = overall + jnp.log(summed)
    copies = broadcast(second_out, second_in, my_row, x2_send, x2_recv, row_n, row_peer)
    second_in[my_row] = second_out[...]
    for copy in copies:
        copy.wait()
    overall = second_in[0]
    for other in range(1, row_n):
        overall = jnp.maximum(overall, second_in[other])
    summed = jnp.zeros_like(overall)
    for other in range(row_n):
        summed = summed + jnp.exp(second_in[other] - overall)
    tpot_one[...] = 0.5 * (log_sources - log_targets) - 0.5 * (overall + jnp.log(summed))
    inverse = float(sources_all) / summed
    for chunk in range(chunks):
        scales[chunk] = jnp.exp(peaks[chunk] - overall) * inverse

    def half_two(chunk, unused):
        at = chunk_rows(chunk)
        total = block[at, lanes(0)] * scales[chunk, 0:1, :]
        for tile in range(1, tiles):
            total = total + block[at, lanes(tile)] * scales[chunk, tile : tile + 1, :]
        third_out[pl.ds(chunk, 1), :] = jnp.sum(total.T, axis=0, keepdims=True)
        return unused

    lax.fori_loop(0, chunks, half_two, 0)
    copies = broadcast(third_out, third_in, my_col, x3_send, x3_recv, col_n, col_peer)
    third_in[my_col] = third_out[...]
    for copy in copies:
        copy.wait()
    summed = third_in[0]
    for other in range(1, col_n):
        summed = summed + third_in[other]
    spot_ref[...] = source_norm[...] + log_targets - 0.5 * (lse[...] + jnp.log(summed))
    lse[...] = float(targets_all) / summed

    column_acc[...] = jnp.zeros_like(column_acc)

    def half_three(chunk, unused):
        at = chunk_rows(chunk)
        weight = spread(lse[pl.ds(chunk, 1), :])
        for tile in range(tiles):
            weighted = (block[at, lanes(tile)] * weight).reshape(CHUNK // 8, 8, LANES)
            column_acc[tile] += jnp.sum(weighted, axis=0) * scales[chunk, tile : tile + 1, :]
        return unused

    lax.fori_loop(0, chunks, half_three, 0)
    fourth_out[...] = jnp.sum(column_acc[...], axis=1)
    copies = broadcast(fourth_out, fourth_in, my_row, x4_send, x4_recv, row_n, row_peer)
    fourth_in[my_row] = fourth_out[...]
    for copy in copies:
        copy.wait()
    summed = fourth_in[0]
    for other in range(1, row_n):
        summed = summed + fourth_in[other]
    tpot_ref[...] = tpot_one[...] + 0.5 * log_sources - 0.5 * jnp.log(summed)


def local(source, target):
    row_n, col_n = lax.axis_size("row"), lax.axis_size("col")
    src_piece, depth = source.shape
    tgt_piece = target.shape[0]
    rows, cols = src_piece * col_n, tgt_piece * row_n
    chunks, tiles = rows // CHUNK, cols // LANES
    f32, bf16 = jnp.float32, jnp.bfloat16
    vmem = pl.BlockSpec(memory_space=pltpu.VMEM)
    row_sems, col_sems = pltpu.SemaphoreType.DMA((row_n - 1,)), pltpu.SemaphoreType.DMA((col_n - 1,))
    spot, tpot = pl.pallas_call(
        functools.partial(kernel, row_n, col_n),
        out_shape=(
            jax.ShapeDtypeStruct((chunks, LANES), f32),
            jax.ShapeDtypeStruct((tiles, LANES), f32),
        ),
        in_specs=[vmem, vmem],
        out_specs=(vmem, vmem),
        scratch_shapes=[
            pltpu.VMEM((col_n, depth, src_piece), bf16),
            pltpu.VMEM((row_n, depth, tgt_piece), bf16),
            pltpu.VMEM((rows, 3 * depth), bf16),
            pltpu.VMEM((3 * depth, cols), bf16),
            pltpu.VMEM((src_piece, LANES), f32),
            pltpu.VMEM((rows, cols), f32),
            pltpu.VMEM((chunks, tiles, LANES), f32),
            pltpu.VMEM((chunks, tiles, LANES), f32),
            pltpu.VMEM((chunks, tiles, LANES), f32),
            pltpu.VMEM((tiles, 8, LANES), f32),
            pltpu.VMEM((chunks, LANES), f32),
            pltpu.VMEM((chunks, LANES), f32),
            pltpu.VMEM((tiles, LANES), f32),
            pltpu.VMEM((col_n, src_piece // CHUNK, LANES), f32),
            pltpu.VMEM((col_n, col_n, src_piece // CHUNK, LANES), f32),
            pltpu.VMEM((tiles, LANES), f32),
            pltpu.VMEM((row_n, tiles, LANES), f32),
            pltpu.VMEM((chunks, LANES), f32),
            pltpu.VMEM((col_n, chunks, LANES), f32),
            pltpu.VMEM((tiles, LANES), f32),
            pltpu.VMEM((row_n, tiles, LANES), f32),
            col_sems, pltpu.SemaphoreType.DMA((col_n,)), row_sems, row_sems,
            pltpu.SemaphoreType.DMA((col_n - 1, col_n)), pltpu.SemaphoreType.DMA((col_n, col_n)), row_sems, row_sems,
            col_sems, col_sems, row_sems, row_sems,
        ],
        compiler_params=pltpu.CompilerParams(
            collective_id=0, has_side_effects=True, vmem_limit_bytes=48 * 1024 * 1024
        ),
    )(source.T, target.T)
    return spot.reshape(-1), tpot.reshape(-1)


def solution(mesh):
    placed = (P(("row", "col"), None), P(("col", "row"), None))
    return jax.shard_map(
        local, mesh=mesh, in_specs=placed, out_specs=(P("row"), P("col")), check_vma=False
    )
```

```python
import functools
import math

import jax
import jax.numpy as jnp
from jax import lax
from jax.experimental import pallas as pl
from jax.experimental.pallas import tpu as pltpu
from jax.sharding import PartitionSpec as P

MESH = pl.DeviceIdType.MESH
CHUNK = 128
LANES = 128
NN_DIMS = (((1,), (0,)), ((), ()))


def spread(row):
    return jnp.broadcast_to(row, (CHUNK, LANES)).T


def exact_pieces(squared):
    high = squared.astype(jnp.bfloat16)
    low = (squared - high.astype(jnp.float32)).astype(jnp.bfloat16)
    return high, low


def kernel(
    row_n, col_n, src_ref, tgt_ref, spot_ref, tpot_ref,
    src_all, tgt_all, left, right, tops, row_acc, block, peaks, sums, scales, column_acc, lse, source_norm, tpot_one,
    first_out, first_in, second_out, second_in, third_out, third_in, fourth_out, fourth_in,
    src_send, src_recv, tgt_send, tgt_recv, x1_send, x1_recv, x2_send, x2_recv, x3_send, x3_recv, x4_send, x4_recv,
):
    my_row, my_col = lax.axis_index("row"), lax.axis_index("col")
    depth, src_piece = src_ref.shape
    tgt_piece = tgt_ref.shape[1]
    rows, cols = src_piece * col_n, tgt_piece * row_n
    chunks, tiles = rows // CHUNK, cols // LANES
    sources_all, targets_all = rows * row_n, cols * col_n
    log_sources, log_targets = math.log(sources_all), math.log(targets_all)

    def col_peer(step):
        return (my_row, lax.rem(my_col + step, col_n))

    def nearest(step):
        below, above = my_col, col_n - 1 - my_col
        low_side = lax.div(above - below + col_n, col_n)
        reach = low_side * below + (1 - low_side) * above
        both = lax.div(2 * reach - step + col_n, col_n)
        around = (step + 1) // 2 * (2 * (step % 2) - 1)
        return my_col + both * around + (1 - both) * (step - reach) * (2 * low_side - 1)

    def near_peer(step):
        return (my_row, nearest(step))

    def row_peer(step):
        return (lax.rem(my_row + step, row_n), my_col)

    barrier = pltpu.get_barrier_semaphore()
    for step in range(1, row_n):
        pl.semaphore_signal(barrier, inc=1, device_id=row_peer(step), device_id_type=MESH)
    for step in range(1, col_n):
        pl.semaphore_signal(barrier, inc=1, device_id=col_peer(step), device_id_type=MESH)
    src_all[my_col] = src_ref[...]
    tgt_all[my_row] = tgt_ref[...]
    left[:, depth : 3 * depth] = jnp.full((rows, 2 * depth), -2.0, jnp.bfloat16)
    pl.semaphore_wait(barrier, row_n + col_n - 2)

    def broadcast(source, landing, slot, send, recv, count, peer):
        copies = []
        for step in range(1, count):
            copy = pltpu.make_async_remote_copy(
                src_ref=source,
                dst_ref=landing.at[slot],
                send_sem=send.at[step - 1],
                recv_sem=recv.at[step - 1],
                device_id=peer(step),
                device_id_type=MESH,
            )
            copy.start()
            copies.append(copy)
        return copies

    def send_all(source, target, send, recv, count, peer):
        copies = []
        for step in range(1, count):
            copy = pltpu.make_async_remote_copy(
                src_ref=source,
                dst_ref=target,
                send_sem=send(step - 1),
                recv_sem=recv,
                device_id=peer(step),
                device_id_type=MESH,
            )
            copy.start()
            copies.append(copy)
        return copies

    src_copies = send_all(
        src_ref, src_all.at[my_col], lambda k: src_send.at[k], src_recv.at[my_col], col_n, near_peer
    )
    tgt_copies = broadcast(tgt_ref, tgt_all, my_row, tgt_send, tgt_recv, row_n, row_peer)
    for copy in tgt_copies:
        copy.wait()

    for piece in range(row_n):
        wide = tgt_all[piece].astype(jnp.float32)
        high, low = exact_pieces(wide * wide)
        at = slice(piece * tgt_piece, (piece + 1) * tgt_piece)
        right[0:depth, at] = tgt_all[piece]
        right[depth : 2 * depth, at] = high
        right[2 * depth : 3 * depth, at] = low

    def chunk_rows(chunk):
        return pl.ds(pl.multiple_of(chunk * CHUNK, CHUNK), CHUNK)

    def lanes(tile):
        return slice(tile * LANES, (tile + 1) * LANES)

    piece_chunks = src_piece // CHUNK
    width = math.gcd(cols, 512)

    def half_zero(piece):
        wide = src_all[piece].astype(jnp.float32)
        at = pl.ds(pl.multiple_of(piece * src_piece, src_piece), src_piece)
        left[at, 0:depth] = (4.0 * wide).T.astype(jnp.bfloat16)
        norm = jnp.sum(wide * wide, axis=0, keepdims=True)
        for part in range(piece_chunks):
            source_norm[pl.ds(piece * piece_chunks + part, 1), :] = norm[:, lanes(part)]
        top = None
        for group in range(cols // width):
            at_cols = slice(group * width, (group + 1) * width)
            score = lax.dot_general(
                left[at, :], right[:, at_cols], NN_DIMS, preferred_element_type=jnp.float32
            )
            block[at, at_cols] = score
            for tile in range(width // LANES):
                part = score[:, lanes(tile)]
                top = part if top is None else jnp.maximum(top, part)
        tops[...] = top

        def exponentials(part, unused):
            at = chunk_rows(piece * piece_chunks + part)
            top = tops[chunk_rows(part), :]
            highest = jnp.max(top, axis=1, keepdims=True)
            total = jnp.exp(block[at, lanes(0)] - highest)
            for tile in range(1, tiles):
                total = total + jnp.exp(block[at, lanes(tile)] - highest)
            first_out[piece, pl.ds(part, 1), :] = jnp.max(top.T, axis=0, keepdims=True) + jnp.log(
                jnp.sum(total.T, axis=0, keepdims=True)
            )
            return unused

        lax.fori_loop(0, piece_chunks, exponentials, 0)
        send_all(
            first_out.at[piece], first_in.at[my_col, piece],
            lambda k: x1_send.at[k, piece], x1_recv.at[my_col, piece], col_n, col_peer,
        )
        first_in[my_col, piece] = first_out[piece]

    half_zero(my_col)

    def other_piece(step, unused):
        piece = nearest(step)
        pltpu.make_async_remote_copy(
            src_ref=src_ref,
            dst_ref=src_all.at[piece],
            send_sem=src_send.at[0],
            recv_sem=src_recv.at[piece],
            device_id=col_peer(1),
            device_id_type=MESH,
        ).wait_recv()
        half_zero(piece)
        return unused

    lax.fori_loop(1, col_n, other_piece, 0)
    for copy in src_copies:
        copy.wait_send()

    half_tiles, half_chunks = tiles // 2, chunks // 2

    def first_copy(step, sender, piece):
        return pltpu.make_async_remote_copy(
            src_ref=first_out.at[piece],
            dst_ref=first_in.at[sender, piece],
            send_sem=x1_send.at[step - 1, piece],
            recv_sem=x1_recv.at[sender, piece],
            device_id=col_peer(step),
            device_id_type=MESH,
        )

    def finish_rows(place, unused):
        piece = (col_n - 1) // 2 + (place + 1) // 2 * (2 * (place % 2) - 1)
        for step in range(1, col_n):
            first_copy(step, lax.rem(my_col + step, col_n), piece).wait()
        overall = first_in[0, piece]
        for other in range(1, col_n):
            overall = jnp.maximum(overall, first_in[other, piece])
        summed = jnp.zeros_like(overall)
        for other in range(col_n):
            summed = summed + jnp.exp(first_in[other, piece] - overall)
        total = overall + jnp.log(summed)
        for part in range(piece_chunks):
            lse[pl.ds(piece * piece_chunks + part, 1), :] = total[part : part + 1, :]
        lax.fori_loop(piece * piece_chunks, (piece + 1) * piece_chunks, functools.partial(half_one, 0), 0)
        return unused

    def half_one(group, chunk, unused):
        at = chunk_rows(chunk)
        shift = spread(lse[pl.ds(chunk, 1), :])
        for tile in range(group * half_tiles, (group + 1) * half_tiles):
            shifted = block[at, lanes(tile)] - shift
            highest = jnp.max(shifted, axis=0, keepdims=True)
            value = jnp.exp(shifted - highest)
            block[at, lanes(tile)] = value
            peaks[chunk, tile : tile + 1, :] = highest
            sums[chunk, tile : tile + 1, :] = jnp.sum(value, axis=0, keepdims=True)
        return unused

    lax.fori_loop(0, col_n, finish_rows, 0)
    def group_tiles(group):
        return slice(group * half_tiles, (group + 1) * half_tiles)

    def start_columns(group):
        at = group_tiles(group)
        overall = peaks[0, at]
        for chunk in range(1, chunks):
            overall = jnp.maximum(overall, peaks[chunk, at])
        summed = jnp.zeros_like(overall)
        for chunk in range(chunks):
            summed = summed + sums[chunk, at] * jnp.exp(peaks[chunk, at] - overall)
        result = overall + jnp.log(summed)
        second_out[at, :] = result
        second_in[my_row, at, :] = result
        return send_all(
            second_out.at[at], second_in.at[my_row, at],
            lambda k: x2_send.at[group, k], x2_recv.at[group, my_row], row_n, row_peer,
        )

    def wait_from(group, source, landing, send, recv, count, mine, peer, copies):
        for copy in copies:
            copy.wait_send()
        for step in range(1, count):
            sender = lax.rem(mine + step, count)
            pltpu.make_async_remote_copy(
                src_ref=source, dst_ref=landing(sender), send_sem=send.at[group, 0], recv_sem=recv.at[group, sender],
                device_id=peer(step), device_id_type=MESH,
            ).wait_recv()

    def finish_columns(group, copies):
        at = group_tiles(group)
        wait_from(
            group, second_out.at[at], lambda sender: second_in.at[sender, at],
            x2_send, x2_recv, row_n, my_row, row_peer, copies,
        )
        overall = second_in[0, at]
        for other in range(1, row_n):
            overall = jnp.maximum(overall, second_in[other, at])
        summed = jnp.zeros_like(overall)
        for other in range(row_n):
            summed = summed + jnp.exp(second_in[other, at] - overall)
        tpot_one[at, :] = 0.5 * (log_sources - log_targets) - 0.5 * (overall + jnp.log(summed))
        inverse = float(sources_all) / summed
        for chunk in range(chunks):
            scales[chunk, at, :] = jnp.exp(peaks[chunk, at] - overall) * inverse

    def partial_row(chunk, group):
        at = chunk_rows(chunk)
        total = None
        for tile in range(group * half_tiles, (group + 1) * half_tiles):
            term = block[at, lanes(tile)] * scales[chunk, tile : tile + 1, :]
            total = term if total is None else total + term
        return total

    def half_two_first(chunk, unused):
        row_acc[chunk_rows(chunk), :] = partial_row(chunk, 0)
        return unused

    def half_two(chunk, unused):
        total = row_acc[chunk_rows(chunk), :] + partial_row(chunk, 1)
        third_out[pl.ds(chunk, 1), :] = jnp.sum(total.T, axis=0, keepdims=True)
        return unused

    first_columns = start_columns(0)
    lax.fori_loop(0, chunks, functools.partial(half_one, 1), 0)
    second_columns = start_columns(1)
    finish_columns(0, first_columns)
    lax.fori_loop(0, chunks, half_two_first, 0)
    finish_columns(1, second_columns)

    def group_chunks(group):
        return slice(group * half_chunks, (group + 1) * half_chunks)

    row_copies = []
    for group in range(2):
        at = group_chunks(group)
        lax.fori_loop(group * half_chunks, (group + 1) * half_chunks, half_two, 0)
        third_in[my_col, at, :] = third_out[at, :]
        row_copies.append(
            send_all(
                third_out.at[at], third_in.at[my_col, at],
                lambda k, group=group: x3_send.at[group, k], x3_recv.at[group, my_col], col_n, col_peer,
            )
        )

    column_acc[...] = jnp.zeros_like(column_acc)

    def half_three(chunk, unused):
        at = chunk_rows(chunk)
        weight = spread(lse[pl.ds(chunk, 1), :])
        for tile in range(tiles):
            weighted = (block[at, lanes(tile)] * weight).reshape(CHUNK // 8, 8, LANES)
            column_acc[tile] += jnp.sum(weighted, axis=0) * scales[chunk, tile : tile + 1, :]
        return unused

    for group in range(2):
        at = group_chunks(group)
        wait_from(
            group, third_out.at[at], lambda sender, at=at: third_in.at[sender, at],
            x3_send, x3_recv, col_n, my_col, col_peer, row_copies[group],
        )
        summed = third_in[0, at]
        for other in range(1, col_n):
            summed = summed + third_in[other, at]
        spot_ref[at, :] = source_norm[at, :] + log_targets - 0.5 * (lse[at, :] + jnp.log(summed))
        lse[at, :] = float(targets_all) / summed
        lax.fori_loop(group * half_chunks, (group + 1) * half_chunks, half_three, 0)
    fourth_out[...] = jnp.sum(column_acc[...], axis=1)
    copies = broadcast(fourth_out, fourth_in, my_row, x4_send, x4_recv, row_n, row_peer)
    fourth_in[my_row] = fourth_out[...]
    for copy in copies:
        copy.wait()
    summed = fourth_in[0]
    for other in range(1, row_n):
        summed = summed + fourth_in[other]
    tpot_ref[...] = tpot_one[...] + 0.5 * log_sources - 0.5 * jnp.log(summed)


def local(source, target):
    row_n, col_n = lax.axis_size("row"), lax.axis_size("col")
    src_piece, depth = source.shape
    tgt_piece = target.shape[0]
    rows, cols = src_piece * col_n, tgt_piece * row_n
    chunks, tiles = rows // CHUNK, cols // LANES
    f32, bf16 = jnp.float32, jnp.bfloat16
    vmem = pl.BlockSpec(memory_space=pltpu.VMEM)
    row_sems, col_sems = pltpu.SemaphoreType.DMA((row_n - 1,)), pltpu.SemaphoreType.DMA((col_n - 1,))
    spot, tpot = pl.pallas_call(
        functools.partial(kernel, row_n, col_n),
        out_shape=(
            jax.ShapeDtypeStruct((chunks, LANES), f32),
            jax.ShapeDtypeStruct((tiles, LANES), f32),
        ),
        in_specs=[vmem, vmem],
        out_specs=(vmem, vmem),
        scratch_shapes=[
            pltpu.VMEM((col_n, depth, src_piece), bf16),
            pltpu.VMEM((row_n, depth, tgt_piece), bf16),
            pltpu.VMEM((rows, 3 * depth), bf16),
            pltpu.VMEM((3 * depth, cols), bf16),
            pltpu.VMEM((src_piece, LANES), f32),
            pltpu.VMEM((rows, LANES), f32),
            pltpu.VMEM((rows, cols), f32),
            pltpu.VMEM((chunks, tiles, LANES), f32),
            pltpu.VMEM((chunks, tiles, LANES), f32),
            pltpu.VMEM((chunks, tiles, LANES), f32),
            pltpu.VMEM((tiles, 8, LANES), f32),
            pltpu.VMEM((chunks, LANES), f32),
            pltpu.VMEM((chunks, LANES), f32),
            pltpu.VMEM((tiles, LANES), f32),
            pltpu.VMEM((col_n, src_piece // CHUNK, LANES), f32),
            pltpu.VMEM((col_n, col_n, src_piece // CHUNK, LANES), f32),
            pltpu.VMEM((tiles, LANES), f32),
            pltpu.VMEM((row_n, tiles, LANES), f32),
            pltpu.VMEM((chunks, LANES), f32),
            pltpu.VMEM((col_n, chunks, LANES), f32),
            pltpu.VMEM((tiles, LANES), f32),
            pltpu.VMEM((row_n, tiles, LANES), f32),
            col_sems, pltpu.SemaphoreType.DMA((col_n,)), row_sems, row_sems,
            pltpu.SemaphoreType.DMA((col_n - 1, col_n)), pltpu.SemaphoreType.DMA((col_n, col_n)),
            pltpu.SemaphoreType.DMA((2, row_n - 1)), pltpu.SemaphoreType.DMA((2, row_n)),
            pltpu.SemaphoreType.DMA((2, col_n - 1)), pltpu.SemaphoreType.DMA((2, col_n)),
            row_sems, row_sems,
        ],
        compiler_params=pltpu.CompilerParams(
            collective_id=0, has_side_effects=True, vmem_limit_bytes=48 * 1024 * 1024
        ),
    )(source.T, target.T)
    return spot.reshape(-1), tpot.reshape(-1)


def solution(mesh):
    placed = (P(("row", "col"), None), P(("col", "row"), None))
    return jax.shard_map(
        local, mesh=mesh, in_specs=placed, out_specs=(P("row"), P("col")), check_vma=False
    )
```

```python
import functools
import math

import jax
import jax.numpy as jnp
from jax import lax
from jax.experimental import pallas as pl
from jax.experimental.pallas import tpu as pltpu
from jax.sharding import PartitionSpec as P

MESH = pl.DeviceIdType.MESH
CHUNK = 128
LANES = 128
NN_DIMS = (((1,), (0,)), ((), ()))


def spread(row):
    return jnp.broadcast_to(row, (CHUNK, LANES)).T


def exact_pieces(squared):
    high = squared.astype(jnp.bfloat16)
    low = (squared - high.astype(jnp.float32)).astype(jnp.bfloat16)
    return high, low


def kernel(
    row_n, col_n, src_ref, tgt_ref, spot_ref, tpot_ref,
    src_all, tgt_all, left, right, tops, block, peaks, sums, scales, column_acc, lse, source_norm, tpot_one,
    first_out, first_in, second_out, second_in, third_out, third_in, fourth_out, fourth_in,
    src_send, src_recv, tgt_send, tgt_recv, x1_send, x1_recv, x2_send, x2_recv, x3_send, x3_recv, x4_send, x4_recv,
):
    my_row, my_col = lax.axis_index("row"), lax.axis_index("col")
    depth, src_piece = src_ref.shape
    tgt_piece = tgt_ref.shape[1]
    rows, cols = src_piece * col_n, tgt_piece * row_n
    chunks, tiles = rows // CHUNK, cols // LANES
    sources_all, targets_all = rows * row_n, cols * col_n
    log_sources, log_targets = math.log(sources_all), math.log(targets_all)

    def col_peer(step):
        return (my_row, lax.rem(my_col + step, col_n))

    def nearest(step):
        below, above = my_col, col_n - 1 - my_col
        low_side = lax.div(above - below + col_n, col_n)
        reach = low_side * below + (1 - low_side) * above
        both = lax.div(2 * reach - step + col_n, col_n)
        around = (step + 1) // 2 * (2 * (step % 2) - 1)
        return my_col + both * around + (1 - both) * (step - reach) * (2 * low_side - 1)

    def near_peer(step):
        return (my_row, nearest(step))

    def row_peer(step):
        return (lax.rem(my_row + step, row_n), my_col)

    barrier = pltpu.get_barrier_semaphore()
    for step in range(1, row_n):
        pl.semaphore_signal(barrier, inc=1, device_id=row_peer(step), device_id_type=MESH)
    for step in range(1, col_n):
        pl.semaphore_signal(barrier, inc=1, device_id=col_peer(step), device_id_type=MESH)
    src_all[my_col] = src_ref[...]
    tgt_all[my_row] = tgt_ref[...]
    left[:, depth : 3 * depth] = jnp.full((rows, 2 * depth), -2.0, jnp.bfloat16)
    pl.semaphore_wait(barrier, row_n + col_n - 2)

    def broadcast(source, landing, slot, send, recv, count, peer):
        copies = []
        for step in range(1, count):
            copy = pltpu.make_async_remote_copy(
                src_ref=source,
                dst_ref=landing.at[slot],
                send_sem=send.at[step - 1],
                recv_sem=recv.at[step - 1],
                device_id=peer(step),
                device_id_type=MESH,
            )
            copy.start()
            copies.append(copy)
        return copies

    def send_all(source, target, send, recv, count, peer, first=1):
        copies = []
        for step in range(first, count):
            copy = pltpu.make_async_remote_copy(
                src_ref=source,
                dst_ref=target,
                send_sem=send(step - 1),
                recv_sem=recv,
                device_id=peer(step),
                device_id_type=MESH,
            )
            copy.start()
            copies.append(copy)
        return copies

    near_n = col_n // 2 + 1
    src_copies = send_all(
        src_ref, src_all.at[my_col], lambda k: src_send.at[k], src_recv.at[my_col], near_n, near_peer
    )
    tgt_copies = broadcast(tgt_ref, tgt_all, my_row, tgt_send, tgt_recv, row_n, row_peer)
    for copy in tgt_copies:
        copy.wait()
    src_copies += send_all(
        src_ref, src_all.at[my_col], lambda k: src_send.at[k], src_recv.at[my_col], col_n, near_peer, near_n
    )

    for piece in range(row_n):
        wide = tgt_all[piece].astype(jnp.float32)
        high, low = exact_pieces(wide * wide)
        at = slice(piece * tgt_piece, (piece + 1) * tgt_piece)
        right[0:depth, at] = tgt_all[piece]
        right[depth : 2 * depth, at] = high
        right[2 * depth : 3 * depth, at] = low

    def chunk_rows(chunk):
        return pl.ds(pl.multiple_of(chunk * CHUNK, CHUNK), CHUNK)

    def lanes(tile):
        return slice(tile * LANES, (tile + 1) * LANES)

    piece_chunks = src_piece // CHUNK
    width = math.gcd(cols, 512)

    def half_zero(piece):
        wide = src_all[piece].astype(jnp.float32)
        at = pl.ds(pl.multiple_of(piece * src_piece, src_piece), src_piece)
        left[at, 0:depth] = (4.0 * wide).T.astype(jnp.bfloat16)
        norm = jnp.sum(wide * wide, axis=0, keepdims=True)
        for part in range(piece_chunks):
            source_norm[pl.ds(piece * piece_chunks + part, 1), :] = norm[:, lanes(part)]
        top = None
        for group in range(cols // width):
            at_cols = slice(group * width, (group + 1) * width)
            score = lax.dot_general(
                left[at, :], right[:, at_cols], NN_DIMS, preferred_element_type=jnp.float32
            )
            block[at, at_cols] = score
            for tile in range(width // LANES):
                part = score[:, lanes(tile)]
                top = part if top is None else jnp.maximum(top, part)
        tops[...] = top

        def exponentials(part, unused):
            at = chunk_rows(piece * piece_chunks + part)
            top = tops[chunk_rows(part), :]
            highest = jnp.max(top, axis=1, keepdims=True)
            total = jnp.exp(block[at, lanes(0)] - highest)
            for tile in range(1, tiles):
                total = total + jnp.exp(block[at, lanes(tile)] - highest)
            first_out[piece, pl.ds(part, 1), :] = jnp.max(top.T, axis=0, keepdims=True) + jnp.log(
                jnp.sum(total.T, axis=0, keepdims=True)
            )
            return unused

        lax.fori_loop(0, piece_chunks, exponentials, 0)
        send_all(
            first_out.at[piece], first_in.at[my_col, piece],
            lambda k: x1_send.at[k, piece], x1_recv.at[my_col, piece], col_n, col_peer,
        )
        first_in[my_col, piece] = first_out[piece]

    half_zero(my_col)

    def other_piece(step, unused):
        piece = nearest(step)
        pltpu.make_async_remote_copy(
            src_ref=src_ref,
            dst_ref=src_all.at[piece],
            send_sem=src_send.at[0],
            recv_sem=src_recv.at[piece],
            device_id=col_peer(1),
            device_id_type=MESH,
        ).wait_recv()
        half_zero(piece)
        return unused

    lax.fori_loop(1, col_n, other_piece, 0)
    for copy in src_copies:
        copy.wait_send()

    def first_copy(step, sender, piece):
        return pltpu.make_async_remote_copy(
            src_ref=first_out.at[piece],
            dst_ref=first_in.at[sender, piece],
            send_sem=x1_send.at[step - 1, piece],
            recv_sem=x1_recv.at[sender, piece],
            device_id=col_peer(step),
            device_id_type=MESH,
        )

    def finish_rows(place, unused):
        piece = (col_n - 1) // 2 + (place + 1) // 2 * (2 * (place % 2) - 1)
        for step in range(1, col_n):
            first_copy(step, lax.rem(my_col + step, col_n), piece).wait()
        overall = first_in[0, piece]
        for other in range(1, col_n):
            overall = jnp.maximum(overall, first_in[other, piece])
        summed = jnp.zeros_like(overall)
        for other in range(col_n):
            summed = summed + jnp.exp(first_in[other, piece] - overall)
        total = overall + jnp.log(summed)
        for part in range(piece_chunks):
            lse[pl.ds(piece * piece_chunks + part, 1), :] = total[part : part + 1, :]
        lax.fori_loop(piece * piece_chunks, (piece + 1) * piece_chunks, half_one, 0)
        return unused

    def half_one(chunk, unused):
        at = chunk_rows(chunk)
        shift = spread(lse[pl.ds(chunk, 1), :])
        for tile in range(tiles):
            shifted = block[at, lanes(tile)] - shift
            highest = jnp.max(shifted, axis=0, keepdims=True)
            value = jnp.exp(shifted - highest)
            block[at, lanes(tile)] = value
            peaks[chunk, tile : tile + 1, :] = highest
            sums[chunk, tile : tile + 1, :] = jnp.sum(value, axis=0, keepdims=True)
        return unused

    lax.fori_loop(0, col_n, finish_rows, 0)
    overall = peaks[0]
    for chunk in range(1, chunks):
        overall = jnp.maximum(overall, peaks[chunk])
    summed = jnp.zeros_like(overall)
    for chunk in range(chunks):
        summed = summed + sums[chunk] * jnp.exp(peaks[chunk] - overall)
    second_out[...] = overall + jnp.log(summed)
    copies = broadcast(second_out, second_in, my_row, x2_send, x2_recv, row_n, row_peer)
    second_in[my_row] = second_out[...]
    for copy in copies:
        copy.wait()
    overall = second_in[0]
    for other in range(1, row_n):
        overall = jnp.maximum(overall, second_in[other])
    summed = jnp.zeros_like(overall)
    for other in range(row_n):
        summed = summed + jnp.exp(second_in[other] - overall)
    tpot_one[...] = 0.5 * (log_sources - log_targets) - 0.5 * (overall + jnp.log(summed))
    inverse = float(sources_all) / summed
    for chunk in range(chunks):
        scales[chunk] = jnp.exp(peaks[chunk] - overall) * inverse

    def half_two(chunk, unused):
        at = chunk_rows(chunk)
        total = block[at, lanes(0)] * scales[chunk, 0:1, :]
        for tile in range(1, tiles):
            total = total + block[at, lanes(tile)] * scales[chunk, tile : tile + 1, :]
        third_out[pl.ds(chunk, 1), :] = jnp.sum(total.T, axis=0, keepdims=True)
        return unused

    lax.fori_loop(0, chunks, half_two, 0)
    copies = broadcast(third_out, third_in, my_col, x3_send, x3_recv, col_n, col_peer)
    third_in[my_col] = third_out[...]
    for copy in copies:
        copy.wait()
    summed = third_in[0]
    for other in range(1, col_n):
        summed = summed + third_in[other]
    spot_ref[...] = source_norm[...] + log_targets - 0.5 * (lse[...] + jnp.log(summed))
    lse[...] = float(targets_all) / summed

    column_acc[...] = jnp.zeros_like(column_acc)

    def half_three(chunk, unused):
        at = chunk_rows(chunk)
        weight = spread(lse[pl.ds(chunk, 1), :])
        for tile in range(tiles):
            weighted = (block[at, lanes(tile)] * weight).reshape(CHUNK // 8, 8, LANES)
            column_acc[tile] += jnp.sum(weighted, axis=0) * scales[chunk, tile : tile + 1, :]
        return unused

    lax.fori_loop(0, chunks, half_three, 0)
    fourth_out[...] = jnp.sum(column_acc[...], axis=1)
    copies = broadcast(fourth_out, fourth_in, my_row, x4_send, x4_recv, row_n, row_peer)
    fourth_in[my_row] = fourth_out[...]
    for copy in copies:
        copy.wait()
    summed = fourth_in[0]
    for other in range(1, row_n):
        summed = summed + fourth_in[other]
    tpot_ref[...] = tpot_one[...] + 0.5 * log_sources - 0.5 * jnp.log(summed)


def local(source, target):
    row_n, col_n = lax.axis_size("row"), lax.axis_size("col")
    src_piece, depth = source.shape
    tgt_piece = target.shape[0]
    rows, cols = src_piece * col_n, tgt_piece * row_n
    chunks, tiles = rows // CHUNK, cols // LANES
    f32, bf16 = jnp.float32, jnp.bfloat16
    vmem = pl.BlockSpec(memory_space=pltpu.VMEM)
    row_sems, col_sems = pltpu.SemaphoreType.DMA((row_n - 1,)), pltpu.SemaphoreType.DMA((col_n - 1,))
    spot, tpot = pl.pallas_call(
        functools.partial(kernel, row_n, col_n),
        out_shape=(
            jax.ShapeDtypeStruct((chunks, LANES), f32),
            jax.ShapeDtypeStruct((tiles, LANES), f32),
        ),
        in_specs=[vmem, vmem],
        out_specs=(vmem, vmem),
        scratch_shapes=[
            pltpu.VMEM((col_n, depth, src_piece), bf16),
            pltpu.VMEM((row_n, depth, tgt_piece), bf16),
            pltpu.VMEM((rows, 3 * depth), bf16),
            pltpu.VMEM((3 * depth, cols), bf16),
            pltpu.VMEM((src_piece, LANES), f32),
            pltpu.VMEM((rows, cols), f32),
            pltpu.VMEM((chunks, tiles, LANES), f32),
            pltpu.VMEM((chunks, tiles, LANES), f32),
            pltpu.VMEM((chunks, tiles, LANES), f32),
            pltpu.VMEM((tiles, 8, LANES), f32),
            pltpu.VMEM((chunks, LANES), f32),
            pltpu.VMEM((chunks, LANES), f32),
            pltpu.VMEM((tiles, LANES), f32),
            pltpu.VMEM((col_n, src_piece // CHUNK, LANES), f32),
            pltpu.VMEM((col_n, col_n, src_piece // CHUNK, LANES), f32),
            pltpu.VMEM((tiles, LANES), f32),
            pltpu.VMEM((row_n, tiles, LANES), f32),
            pltpu.VMEM((chunks, LANES), f32),
            pltpu.VMEM((col_n, chunks, LANES), f32),
            pltpu.VMEM((tiles, LANES), f32),
            pltpu.VMEM((row_n, tiles, LANES), f32),
            col_sems, pltpu.SemaphoreType.DMA((col_n,)), row_sems, row_sems,
            pltpu.SemaphoreType.DMA((col_n - 1, col_n)), pltpu.SemaphoreType.DMA((col_n, col_n)), row_sems, row_sems,
            col_sems, col_sems, row_sems, row_sems,
        ],
        compiler_params=pltpu.CompilerParams(
            collective_id=0, has_side_effects=True, vmem_limit_bytes=48 * 1024 * 1024
        ),
    )(source.T, target.T)
    return spot.reshape(-1), tpot.reshape(-1)


def solution(mesh):
    placed = (P(("row", "col"), None), P(("col", "row"), None))
    return jax.shard_map(
        local, mesh=mesh, in_specs=placed, out_specs=(P("row"), P("col")), check_vma=False
    )
```
